32 devices in a mesh: lon: 16 (over z, y, core), lat: 2 (over x).
Axes of the slice: x: 2, y: 2, z: 4, core: 2. Of those that a mesh axis runs over, the one named last changes fastest.
Arguments:
- concentration: float32 [128, 448, 128], P('lon', 'lat'), may hold values from -6 to 6
- wind: bfloat16 [3, 128, 448, 128], P(None, 'lon', 'lat'), may hold values from -0.099609375 to 0.099609375
- kappa: bfloat16 [128, 448, 128], P('lon', 'lat'), may hold values from 0.0099487305 to 0.059814453
- observed: bfloat16 [128, 448, 128], P('lon', 'lat'), may hold values from -6 to 6
Outputs:
- grad_conc: float32 [128, 448, 128], P('lon', 'lat')
- grad_kappa: float32 [128, 448, 128], P('lon', 'lat')
The draws below stay inside these ranges and needn't reach their ends.
All inputs are finite; a program needn't handle non-finite values.
Results may differ from the reference program's by a relative error of at most 0.0023.
Values may be sent and summed in bfloat16 or wider, within the bound.
A program may use at most 128 MiB of HBM per device.

```python
import math
import jax
import jax.numpy as jnp
from jax import lax

L = 128
NX = 128
NY = 448


def shard_levels(rng, dims, split, smallest, high):
    level = 1.0
    for dim, shards_of in split:
        draws = jax.random.uniform(jax.random.fold_in(jax.random.fold_in(rng, 6), dim), (shards_of,), jnp.float32, smallest / len(split), high / len(split))
        level = level * jnp.repeat(jnp.exp(draws), dims[dim] // shards_of).reshape((-1,) + (1,) * (len(dims) - 1 - dim))
    return level


def normal_values(stream_key, extent, scale, limit, cuts=(), kind=jnp.bfloat16):
    values = scale * jax.random.normal(stream_key, extent, jnp.float32)
    if cuts:
        values = values * shard_levels(stream_key, extent, cuts, -0.22, 0.18)
    return jnp.clip(values, -limit, limit).astype(kind)


def setup_inputs(seed: int = 0) -> dict:
    splits = jax.random.split(jax.random.key(seed), 5)
    return {
        "concentration": normal_values(splits[0], (NX, NY, L), 1.0, 6.0, ((0, 16), (1, 2)), jnp.float32),
        "wind": jnp.clip(jax.random.uniform(splits[1], (3, NX, NY, L), jnp.float32, -0.099609375, 0.099609375) * shard_levels(splits[1], (3, NX, NY, L), ((1, 16), (2, 2)), -0.4, 0.0), -0.099609375, 0.099609375).astype(jnp.bfloat16),
        "kappa": jnp.clip(jnp.exp(math.log(0.059814453) - 1.7938024 * jax.random.uniform(splits[2], (NX, NY, L), jnp.float32) ** shard_levels(splits[2], (NX, NY, L), ((0, 16), (1, 2)), -0.2, 0.2)), 0.0099487305, 0.059814453).astype(jnp.bfloat16),
        "observed": normal_values(splits[3], (NX, NY, L), 1.0, 6.0, ((0, 16), (1, 2))),
    }


def coefs(speed, diffuse, opened):
    return ((jnp.maximum(speed, 0.0) + diffuse) * opened, (jnp.minimum(speed, 0.0) - diffuse) * opened)


def forward_nexts(field):
    zero_lat = jnp.zeros_like(field[:, :1])
    zero_lev = jnp.zeros_like(field[:, :, :1])
    return (jnp.roll(field, -1, 0), jnp.concatenate([field[:, 1:], zero_lat], 1), jnp.concatenate([field[:, :, 1:], zero_lev], 2))


def westward(faces):
    zero_lat = jnp.zeros_like(faces[1][:, :1])
    zero_lev = jnp.zeros_like(faces[2][:, :, :1])
    return (jnp.roll(faces[0], 1, 0), jnp.concatenate([zero_lat, faces[1][:, :-1]], 1), jnp.concatenate([zero_lev, faces[2][:, :, :-1]], 2))


def advance(conc, table):
    nexts = forward_nexts(conc)
    fluxes = tuple(pair[0] * conc + pair[1] * nearby for pair, nearby in zip(table, nexts))
    wests = westward(fluxes)
    return conc - (fluxes[0] + fluxes[1] + fluxes[2]) + (wests[0] + wests[1] + wests[2]), nexts


def retreat(adjoint, table):
    nexts = forward_nexts(adjoint)
    gaps = tuple(nearby - adjoint for nearby in nexts)
    parts = tuple(pair[1] * gap for pair, gap in zip(table, gaps))
    wests = westward(parts)
    gained = table[0][0] * gaps[0] + table[1][0] * gaps[1] + table[2][0] * gaps[2]
    return adjoint + gained + (wests[0] + wests[1] + wests[2]), gaps


def kappa_term(gaps, conc, nexts, north_open, upper_open):
    return gaps[0] * (conc - nexts[0]) + gaps[1] * (conc - nexts[1]) * north_open + gaps[2] * (conc - nexts[2]) * upper_open


def reference(concentration, wind, kappa, observed):
    speeds = wind.astype(jnp.float32)
    diffuse = kappa.astype(jnp.float32)
    north_open = (lax.broadcasted_iota(jnp.int32, (1, NY, 1), 1) < NY - 1).astype(jnp.float32)
    upper_open = (lax.broadcasted_iota(jnp.int32, (1, 1, L), 2) < L - 1).astype(jnp.float32)
    table = (coefs(speeds[0], diffuse, 1.0), coefs(speeds[1], diffuse, north_open), coefs(speeds[2], diffuse, upper_open))
    middle, nexts_first = advance(concentration, table)
    final, nexts_second = advance(middle, table)
    adjoint = final - observed.astype(jnp.float32)
    adjoint, gaps = retreat(adjoint, table)
    grad_kappa = kappa_term(gaps, middle, nexts_second, north_open, upper_open)
    grad_conc, gaps = retreat(adjoint, table)
    grad_kappa = grad_kappa + kappa_term(gaps, concentration, nexts_first, north_open, upper_open)
    return grad_conc, grad_kappa
```

```python
import functools

import jax
import jax.numpy as jnp
from jax import lax
from jax.experimental import pallas as pl
from jax.experimental.pallas import tpu as pltpu
from jax.sharding import PartitionSpec as P

MESH = pl.DeviceIdType.MESH
PAD = 8
TILE = 16
F32 = jnp.float32
WEST, EAST, SOUTH, NORTH = 0, 1, 2, 3


def kernel(
    lons,
    lats,
    conc_in,
    wind_in,
    kappa_in,
    observed_in,
    grad_conc,
    grad_kappa,
    conc,
    middle,
    lam2,
    lam1,
    own0,
    oth0,
    own1,
    oth1,
    own2,
    oth2,
    wind,
    kappa,
    observed,
    lon_out,
    lon_in,
    lat_out,
    lat_in,
    row_in,
    face_out,
    face_in,
    load_sem,
    send_sem,
    recv_sem,
    early_send,
    early_recv,
):
    rows, cols, levels = conc_in.shape
    lon, lat = lax.axis_index("lon"), lax.axis_index("lat")
    places = (
        {"lon": lax.rem(lon + lons - 1, lons)},
        {"lon": lax.rem(lon + 1, lons)},
        {"lat": lax.rem(lat + lats - 1, lats)},
        {"lat": lax.rem(lat + 1, lats)},
    )
    loads = [
        pltpu.make_async_copy(
            conc_in, conc.at[pl.ds(1, rows), pl.ds(PAD, cols)], load_sem.at[0]
        ),
        pltpu.make_async_copy(kappa_in, kappa, load_sem.at[1]),
        pltpu.make_async_copy(wind_in, wind, load_sem.at[2]),
        pltpu.make_async_copy(observed_in, observed, load_sem.at[3]),
    ]
    for load in loads:
        load.start()

    barrier = pltpu.get_barrier_semaphore()
    for place in places:
        pl.semaphore_signal(barrier, inc=1, device_id=place, device_id_type=MESH)
    pl.semaphore_wait(barrier, 4)

    def remote(source, target, send, recv, place):
        copy = pltpu.make_async_remote_copy(
            src_ref=source,
            dst_ref=target,
            send_sem=send,
            recv_sem=recv,
            device_id=place,
            device_id_type=MESH,
        )
        copy.start()
        return copy

    started = []
    row_copies = [
        remote(
            wind_in.at[0, rows - 1], row_in.at[0], early_send.at[0], early_recv.at[0], places[EAST]
        ),
        remote(
            kappa_in.at[rows - 1], row_in.at[1], early_send.at[1], early_recv.at[1], places[EAST]
        ),
    ]
    started += row_copies

    def send_rims(state, turn):
        inner = pl.ds(PAD, cols)
        lon_out[turn, WEST] = state[1, inner].astype(jnp.bfloat16)
        lon_out[turn, EAST] = state[rows, inner].astype(jnp.bfloat16)
        for i in range(rows):
            lat_out[turn, 0, i : i + 1] = state[i + 1, PAD : PAD + 1]
            lat_out[turn, 1, i : i + 1] = state[i + 1, PAD + cols - 1 : PAD + cols]
        copies = []
        for way in (WEST, EAST):
            copies.append(
                remote(
                    lon_out.at[turn, way],
                    lon_in.at[turn, way],
                    send_sem.at[turn, way],
                    recv_sem.at[turn, way],
                    places[way],
                )
            )
        for way in (SOUTH, NORTH):
            copies.append(
                remote(
                    lat_out.at[turn, way - 2],
                    lat_in.at[turn, way - 2],
                    send_sem.at[turn, way],
                    recv_sem.at[turn, way],
                    places[way],
                )
            )
        started.extend(copies)
        return copies

    north_open = (lat < lats - 1).astype(F32)

    def take_rims(state, turn, copies):
        for copy in copies:
            copy.wait_recv()
        inner = pl.ds(PAD, cols)
        state[rows + 1, inner] = lon_in[turn, WEST].astype(F32)
        state[0, inner] = lon_in[turn, EAST].astype(F32)
        for i in range(rows):
            edge = state[i + 1, PAD + cols - 1 : PAD + cols]
            ghost = lat_in[turn, 0, i : i + 1]
            state[i + 1, PAD + cols : PAD + cols + 1] = edge + (ghost - edge) * north_open
            state[i + 1, PAD - 1 : PAD] = lat_in[turn, 1, i : i + 1]

    def pair(speed, diffuse):
        return jnp.maximum(speed, 0.0) + diffuse, jnp.minimum(speed, 0.0) - diffuse

    def upper(width):
        return (lax.broadcasted_iota(jnp.int32, (width, levels), 1) < levels - 1).astype(F32)

    def chunks(first, last, width, work):
        def one(t, carry):
            work(pl.multiple_of(first + t * width, width))
            return carry

        lax.fori_loop(0, (last - first) // width, one, 0)

    def up(value):
        return pltpu.roll(value, levels - 1, 1)

    def down(value):
        return pltpu.roll(value, 1, 1)

    loads[0].wait()
    copies = send_rims(conc, 0)

    loads[1].wait()
    loads[2].wait()

    def coefs_at(j):
        here = pl.ds(j, TILE)
        padded = pl.ds(pl.multiple_of(j + PAD, 8), TILE)
        shut = upper(TILE)
        for i in range(rows):
            diffuse = kappa[i, here].astype(F32)
            own, oth = pair(wind[0, i, here].astype(F32), diffuse)
            own0[i + 1, here] = own
            oth0[i + 1, here] = oth
            own, oth = pair(wind[1, i, here].astype(F32), diffuse)
            own1[i, padded] = own
            oth1[i, padded] = oth
            own, oth = pair(wind[2, i, here].astype(F32), diffuse)
            own2[i, here] = own * shut
            oth2[i, here] = oth * shut

    chunks(0, cols, TILE, coefs_at)
    last = PAD + cols - 1
    for i in range(rows):
        for place, table in enumerate((own1, oth1)):
            edge = table[i, last : last + 1] * north_open
            table[i, last : last + 1] = edge
            face_out[place, i : i + 1] = edge
    face_copy = remote(face_out, face_in, early_send.at[2], early_recv.at[2], places[NORTH])
    started.append(face_copy)

    def forward(state, target, minus, span, j, width):
        here = pl.ds(j, width)
        mid = pl.multiple_of(j + PAD, 8)
        at, south, north = pl.ds(mid, width), pl.ds(mid - 1, width), pl.ds(mid + 1, width)
        begin = span[0]
        c = state[begin + 1, at]
        f0_west = own0[begin, here] * state[begin, at] + oth0[begin, here] * c
        for i in span:
            east = state[i + 2, at]
            f0 = own0[i + 1, here] * c + oth0[i + 1, here] * east
            f1 = own1[i, at] * c + oth1[i, at] * state[i + 1, north]
            f1_south = own1[i, south] * state[i + 1, south] + oth1[i, south] * c
            f2 = own2[i, here] * c + oth2[i, here] * up(c)
            new = c - (f0 + f1 + f2) + (f0_west + f1_south + down(f2))
            if minus is not None:
                new = new - minus[i, here].astype(F32)
            target[i + 1, at] = new
            f0_west = f0
            c = east

    def backward(state, c_state, target, lead, add, span, j, width):
        here = pl.ds(j, width)
        mid = pl.multiple_of(j + PAD, 8)
        at, south, north = pl.ds(mid, width), pl.ds(mid - 1, width), pl.ds(mid + 1, width)
        spot = here if lead == 0 else at
        shut = upper(width)
        begin = span[0]
        lam = state[begin + 1, at]
        c = c_state[begin + 1, at]
        q0_west = oth0[begin, here] * (lam - state[begin, at])
        for i in span:
            lam_east, c_east = state[i + 2, at], c_state[i + 2, at]
            g0 = lam_east - lam
            g1 = state[i + 1, north] - lam
            g2 = up(lam) - lam
            k = g0 * (c - c_east) + g1 * (c - c_state[i + 1, north]) + g2 * (c - up(c)) * shut
            grad_kappa[i, here] = grad_kappa[i, here] + k if add else k
            gained = own0[i + 1, here] * g0 + own1[i, at] * g1 + own2[i, here] * g2
            q1_south = oth1[i, south] * (lam - state[i + 1, south])
            q2 = oth2[i, here] * g2
            target[i + lead, spot] = lam + gained + (q0_west + q1_south + down(q2))
            q0_west = oth0[i + 1, here] * g0
            lam, c = lam_east, c_east

    inside = tuple(range(1, rows - 1))

    def interior(step):
        chunks(TILE, cols - TILE, TILE, lambda j: step(inside, j, TILE))

    def rim(step):
        def ends(j):
            step((0,), j, TILE)
            step((rows - 1,), j, TILE)

        chunks(0, cols, TILE, ends)
        chunks(0, 2, 1, lambda t: step(inside, pl.multiple_of(t * (cols - TILE), TILE), TILE))

    first = functools.partial(forward, conc, middle, None)
    second = functools.partial(forward, middle, lam2, observed)
    third = functools.partial(backward, lam2, middle, lam1, 1, False)
    fourth = functools.partial(backward, lam1, conc, grad_conc, 0, True)

    interior(first)
    for copy in row_copies + [face_copy]:
        copy.wait_recv()
    own, oth = pair(row_in[0].astype(F32), row_in[1].astype(F32))
    own0[0] = own
    oth0[0] = oth
    for i in range(rows):
        own1[i, PAD - 1 : PAD] = face_in[0, i : i + 1]
        oth1[i, PAD - 1 : PAD] = face_in[1, i : i + 1]
    take_rims(conc, 0, copies)
    rim(first)

    copies = send_rims(middle, 1)
    loads[3].wait()
    interior(second)
    take_rims(middle, 1, copies)
    rim(second)

    copies = send_rims(lam2, 2)
    interior(third)
    take_rims(lam2, 2, copies)
    rim(third)

    copies = send_rims(lam1, 3)
    interior(fourth)
    take_rims(lam1, 3, copies)
    rim(fourth)

    for copy in started:
        copy.wait_send()


def body(lons, lats, concentration, wind, kappa, observed):
    rows, cols, levels = concentration.shape
    state = pltpu.VMEM((rows + 2, cols + 2 * PAD, levels), F32)
    padded = pltpu.VMEM((rows, cols + 2 * PAD, levels), F32)
    wider = pltpu.VMEM((rows + 1, cols, levels), F32)
    plain = pltpu.VMEM((rows, cols, levels), F32)
    out = jax.ShapeDtypeStruct(concentration.shape, F32)
    return pl.pallas_call(
        functools.partial(kernel, lons, lats),
        out_shape=(out, out),
        in_specs=[pl.BlockSpec(memory_space=pl.ANY)] * 4,
        out_specs=(pl.BlockSpec(memory_space=pltpu.VMEM),) * 2,
        scratch_shapes=[
            state,
            state,
            state,
            state,
            wider,
            wider,
            padded,
            padded,
            plain,
            plain,
            pltpu.VMEM(wind.shape, wind.dtype),
            pltpu.VMEM(kappa.shape, kappa.dtype),
            pltpu.VMEM(observed.shape, observed.dtype),
            pltpu.VMEM((4, 2, cols, levels), jnp.bfloat16),
            pltpu.VMEM((4, 2, cols, levels), jnp.bfloat16),
            pltpu.VMEM((4, 2, rows, levels), F32),
            pltpu.VMEM((4, 2, rows, levels), F32),
            pltpu.VMEM((2, cols, levels), jnp.bfloat16),
            pltpu.VMEM((2, rows, levels), F32),
            pltpu.VMEM((2, rows, levels), F32),
            pltpu.SemaphoreType.DMA((4,)),
            pltpu.SemaphoreType.DMA((4, 4)),
            pltpu.SemaphoreType.DMA((4, 4)),
            pltpu.SemaphoreType.DMA((3,)),
            pltpu.SemaphoreType.DMA((3,)),
        ],
        compiler_params=pltpu.CompilerParams(
            collective_id=0, has_side_effects=True, vmem_limit_bytes=60 * 1024 * 1024
        ),
    )(concentration, wind, kappa, observed)


def solution(mesh):
    lons, lats = mesh.shape["lon"], mesh.shape["lat"]
    return jax.shard_map(
        functools.partial(body, lons, lats),
        mesh=mesh,
        in_specs=(
            P("lon", "lat", None),
            P(None, "lon", "lat", None),
            P("lon", "lat", None),
            P("lon", "lat", None),
        ),
        out_specs=(P("lon", "lat", None), P("lon", "lat", None)),
        check_vma=False,
    )
```

```python
import functools

import jax
import jax.numpy as jnp
from jax import lax
from jax.experimental import pallas as pl
from jax.experimental.pallas import tpu as pltpu
from jax.sharding import PartitionSpec as P

MESH = pl.DeviceIdType.MESH
PAD = 8
TILE = 16
F32 = jnp.float32
WEST, EAST, SOUTH, NORTH = 0, 1, 2, 3


def kernel(
    lons,
    lats,
    conc_in,
    wind_in,
    kappa_in,
    observed_in,
    grad_conc,
    grad_kappa,
    conc,
    middle,
    lam2,
    lam1,
    own0,
    oth0,
    own1,
    oth1,
    own2,
    oth2,
    wind,
    kappa,
    observed,
    lon_out,
    lon_in,
    lat_out,
    lat_in,
    row_in,
    face_out,
    face_in,
    load_sem,
    lon_send,
    lon_recv,
    lat_send,
    lat_recv,
    early_send,
    early_recv,
):
    rows, cols, levels = conc_in.shape
    lon, lat = lax.axis_index("lon"), lax.axis_index("lat")
    places = (
        {"lon": lax.rem(lon + lons - 1, lons)},
        {"lon": lax.rem(lon + 1, lons)},
        {"lat": lax.rem(lat + lats - 1, lats)},
        {"lat": lax.rem(lat + 1, lats)},
    )
    loads = [
        pltpu.make_async_copy(
            conc_in, conc.at[pl.ds(1, rows), pl.ds(PAD, cols)], load_sem.at[0]
        ),
        pltpu.make_async_copy(kappa_in, kappa, load_sem.at[1]),
        pltpu.make_async_copy(wind_in, wind, load_sem.at[2]),
        pltpu.make_async_copy(observed_in, observed, load_sem.at[3]),
    ]
    for load in loads:
        load.start()

    barrier = pltpu.get_barrier_semaphore()
    for place in places:
        pl.semaphore_signal(barrier, inc=1, device_id=place, device_id_type=MESH)
    pl.semaphore_wait(barrier, 4)

    def remote(source, target, send, recv, place):
        copy = pltpu.make_async_remote_copy(
            src_ref=source,
            dst_ref=target,
            send_sem=send,
            recv_sem=recv,
            device_id=place,
            device_id_type=MESH,
        )
        copy.start()
        return copy

    started = []
    row_copies = [
        remote(
            wind_in.at[0, rows - 1], row_in.at[0], early_send.at[0], early_recv.at[0], places[EAST]
        ),
        remote(
            kappa_in.at[rows - 1], row_in.at[1], early_send.at[1], early_recv.at[1], places[EAST]
        ),
    ]
    started += row_copies

    half = cols // 2

    def send_lon(state, turn, part):
        inner, there = pl.ds(PAD + part * half, half), pl.ds(part * half, half)
        copies = []
        for way, row in ((EAST, rows), (WEST, 1)):
            lon_out[turn, way, there] = state[row, inner].astype(jnp.bfloat16)
            copies.append(
                remote(
                    lon_out.at[turn, way, there],
                    lon_in.at[turn, way, there],
                    lon_send.at[turn, way, part],
                    lon_recv.at[turn, way, part],
                    places[way],
                )
            )
        started.extend(copies)
        return copies

    def send_lat(state, turn):
        copies = []
        for way, col in ((SOUTH, PAD), (NORTH, PAD + cols - 1)):
            for i in range(rows):
                lat_out[turn, way - 2, i : i + 1] = state[i + 1, col : col + 1]
            copies.append(
                remote(
                    lat_out.at[turn, way - 2],
                    lat_in.at[turn, way - 2],
                    lat_send.at[turn, way - 2],
                    lat_recv.at[turn, way - 2],
                    places[way],
                )
            )
        started.extend(copies)
        return copies

    north_open = (lat < lats - 1).astype(F32)

    def take_lon(state, turn, part, copies):
        for copy in copies:
            copy.wait_recv()
        inner, there = pl.ds(PAD + part * half, half), pl.ds(part * half, half)
        state[rows + 1, inner] = lon_in[turn, WEST, there].astype(F32)
        state[0, inner] = lon_in[turn, EAST, there].astype(F32)

    def take_lat(state, turn, copies):
        for copy in copies:
            copy.wait_recv()
        for i in range(rows):
            edge = state[i + 1, PAD + cols - 1 : PAD + cols]
            ghost = lat_in[turn, 0, i : i + 1]
            state[i + 1, PAD + cols : PAD + cols + 1] = edge + (ghost - edge) * north_open
            state[i + 1, PAD - 1 : PAD] = lat_in[turn, 1, i : i + 1]

    def pair(speed, diffuse):
        return jnp.maximum(speed, 0.0) + diffuse, jnp.minimum(speed, 0.0) - diffuse

    def aligned(start):
        return start if isinstance(start, int) else pl.multiple_of(start, 8)

    def upper(width):
        return (lax.broadcasted_iota(jnp.int32, (width, levels), 1) < levels - 1).astype(F32)

    def chunks(first, last, width, work, most):
        count = (last - first) // width
        group = max(g for g in range(1, most + 1) if count % g == 0)

        def one(t, carry):
            for g in range(group):
                work(pl.multiple_of(first + (t * group + g) * width, width))
            return carry

        if count == group:
            for g in range(group):
                work(first + g * width)
        else:
            lax.fori_loop(0, count // group, one, 0)

    def up(value):
        return pltpu.roll(value, levels - 1, 1)

    def down(value):
        return pltpu.roll(value, 1, 1)

    loads[0].wait()
    lon_copies = [send_lon(conc, 0, part) for part in (0, 1)]
    lat_copies = send_lat(conc, 0)

    loads[1].wait()
    loads[2].wait()

    def coefs_at(j):
        here = pl.ds(j, TILE)
        padded = pl.ds(aligned(j + PAD), TILE)
        shut = upper(TILE)
        for i in range(rows):
            diffuse = kappa[i, here].astype(F32)
            own, oth = pair(wind[0, i, here].astype(F32), diffuse)
            own0[i + 1, here] = own
            oth0[i + 1, here] = oth
            own, oth = pair(wind[1, i, here].astype(F32), diffuse)
            own1[i, padded] = own
            oth1[i, padded] = oth
            own, oth = pair(wind[2, i, here].astype(F32), diffuse)
            own2[i, here] = own * shut
            oth2[i, here] = oth * shut

    chunks(0, cols, TILE, coefs_at, 2)
    last = PAD + cols - 1
    for i in range(rows):
        for place, table in enumerate((own1, oth1)):
            edge = table[i, last : last + 1] * north_open
            table[i, last : last + 1] = edge
            face_out[place, i : i + 1] = edge
    face_copy = remote(face_out, face_in, early_send.at[2], early_recv.at[2], places[NORTH])
    started.append(face_copy)

    def forward(state, target, minus, span, j, width):
        here = pl.ds(j, width)
        mid = aligned(j + PAD)
        at, south, north = pl.ds(mid, width), pl.ds(mid - 1, width), pl.ds(mid + 1, width)
        begin = span[0]
        c = state[begin + 1, at]
        f0_west = own0[begin, here] * state[begin, at] + oth0[begin, here] * c
        for i in span:
            east = state[i + 2, at]
            f0 = own0[i + 1, here] * c + oth0[i + 1, here] * east
            f1 = own1[i, at] * c + oth1[i, at] * state[i + 1, north]
            f1_south = own1[i, south] * state[i + 1, south] + oth1[i, south] * c
            f2 = own2[i, here] * c + oth2[i, here] * up(c)
            new = c - (f0 + f1 + f2) + (f0_west + f1_south + down(f2))
            if minus is not None:
                new = new - minus[i, here].astype(F32)
            target[i + 1, at] = new
            f0_west = f0
            c = east

    def backward(state, c_state, target, lead, add, span, j, width):
        here = pl.ds(j, width)
        mid = aligned(j + PAD)
        at, south, north = pl.ds(mid, width), pl.ds(mid - 1, width), pl.ds(mid + 1, width)
        spot = here if lead == 0 else at
        shut = upper(width)
        begin = span[0]
        lam = state[begin + 1, at]
        c = c_state[begin + 1, at]
        q0_west = oth0[begin, here] * (lam - state[begin, at])
        for i in span:
            lam_east, c_east = state[i + 2, at], c_state[i + 2, at]
            g0 = lam_east - lam
            g1 = state[i + 1, north] - lam
            g2 = up(lam) - lam
            k = g0 * (c - c_east) + g1 * (c - c_state[i + 1, north]) + g2 * (c - up(c)) * shut
            grad_kappa[i, here] = grad_kappa[i, here] + k if add else k
            gained = own0[i + 1, here] * g0 + own1[i, at] * g1 + own2[i, here] * g2
            q1_south = oth1[i, south] * (lam - state[i + 1, south])
            q2 = oth2[i, here] * g2
            target[i + lead, spot] = lam + gained + (q0_west + q1_south + down(q2))
            q0_west = oth0[i + 1, here] * g0
            lam, c = lam_east, c_east

    inside = tuple(range(1, rows - 1))

    def interior(step):
        chunks(TILE, cols - TILE, TILE, lambda j: step(inside, j, TILE), 4)

    def sides(step):
        step(inside, 0, TILE)
        step(inside, cols - TILE, TILE)

    def ends(step, part):
        def both(j):
            step((0,), j, TILE)
            step((rows - 1,), j, TILE)

        chunks(part * half, (part + 1) * half, TILE, both, 7)

    first = functools.partial(forward, conc, middle, None)
    second = functools.partial(forward, middle, lam2, observed)
    third = functools.partial(backward, lam2, middle, lam1, 1, False)
    fourth = functools.partial(backward, lam1, conc, grad_conc, 0, True)

    interior(first)
    face_copy.wait_recv()
    for i in range(rows):
        own1[i, PAD - 1 : PAD] = face_in[0, i : i + 1]
        oth1[i, PAD - 1 : PAD] = face_in[1, i : i + 1]
    take_lat(conc, 0, lat_copies)
    sides(first)
    for copy in row_copies:
        copy.wait_recv()
    own, oth = pair(row_in[0].astype(F32), row_in[1].astype(F32))
    own0[0] = own
    oth0[0] = oth
    for part in (0, 1):
        take_lon(conc, 0, part, lon_copies[part])
        ends(first, part)
        lon_copies[part] = send_lon(middle, 1, part)

    turns = ((middle, second), (lam2, third), (lam1, fourth))
    for turn, (state, step) in enumerate(turns, 1):
        lat_copies = send_lat(state, turn)
        if turn == 1:
            loads[3].wait()
        interior(step)
        take_lat(state, turn, lat_copies)
        sides(step)
        for part in (0, 1):
            take_lon(state, turn, part, lon_copies[part])
            ends(step, part)
            if turn < 3:
                lon_copies[part] = send_lon(turns[turn][0], turn + 1, part)

    for copy in started:
        copy.wait_send()


def body(lons, lats, concentration, wind, kappa, observed):
    rows, cols, levels = concentration.shape
    state = pltpu.VMEM((rows + 2, cols + 2 * PAD, levels), F32)
    padded = pltpu.VMEM((rows, cols + 2 * PAD, levels), F32)
    wider = pltpu.VMEM((rows + 1, cols, levels), F32)
    plain = pltpu.VMEM((rows, cols, levels), F32)
    out = jax.ShapeDtypeStruct(concentration.shape, F32)
    results = pl.pallas_call(
        functools.partial(kernel, lons, lats),
        out_shape=(out, out),
        in_specs=[pl.BlockSpec(memory_space=pl.ANY)] * 4,
        out_specs=(pl.BlockSpec(memory_space=pltpu.VMEM),) * 2,
        scratch_shapes=[
            state,
            state,
            state,
            state,
            wider,
            wider,
            padded,
            padded,
            plain,
            plain,
            pltpu.VMEM(wind.shape, wind.dtype),
            pltpu.VMEM(kappa.shape, kappa.dtype),
            pltpu.VMEM(observed.shape, observed.dtype),
            pltpu.VMEM((4, 2, cols, levels), jnp.bfloat16),
            pltpu.VMEM((4, 2, cols, levels), jnp.bfloat16),
            pltpu.VMEM((4, 2, rows, levels), F32),
            pltpu.VMEM((4, 2, rows, levels), F32),
            pltpu.VMEM((2, cols, levels), jnp.bfloat16),
            pltpu.VMEM((2, rows, levels), F32),
            pltpu.VMEM((2, rows, levels), F32),
            pltpu.SemaphoreType.DMA((4,)),
            pltpu.SemaphoreType.DMA((4, 2, 2)),
            pltpu.SemaphoreType.DMA((4, 2, 2)),
            pltpu.SemaphoreType.DMA((4, 2)),
            pltpu.SemaphoreType.DMA((4, 2)),
            pltpu.SemaphoreType.DMA((3,)),
            pltpu.SemaphoreType.DMA((3,)),
        ],
        compiler_params=pltpu.CompilerParams(
            collective_id=0, has_side_effects=True, vmem_limit_bytes=60 * 1024 * 1024
        ),
    )(concentration, wind, kappa, observed)

    def hand_over(conc_from, kappa_from, conc_to, kappa_to):
        conc_to[...] = conc_from[...]
        kappa_to[...] = kappa_from[...]

    block = pl.BlockSpec((4, cols, levels), lambda i: (i, 0, 0))
    return pl.pallas_call(
        hand_over,
        grid=(rows // 4,),
        out_shape=(out, out),
        in_specs=[block] * 2,
        out_specs=(block,) * 2,
        compiler_params=pltpu.CompilerParams(vmem_limit_bytes=60 * 1024 * 1024),
    )(*results)


def solution(mesh):
    lons, lats = mesh.shape["lon"], mesh.shape["lat"]
    return jax.shard_map(
        functools.partial(body, lons, lats),
        mesh=mesh,
        in_specs=(
            P("lon", "lat", None),
            P(None, "lon", "lat", None),
            P("lon", "lat", None),
            P("lon", "lat", None),
        ),
        out_specs=(P("lon", "lat", None), P("lon", "lat", None)),
        check_vma=False,
    )
```

```python
import functools

import jax
import jax.numpy as jnp
from jax import lax
from jax.experimental import pallas as pl
from jax.experimental.pallas import tpu as pltpu
from jax.sharding import PartitionSpec as P

MESH = pl.DeviceIdType.MESH
PAD = 8
TILE = 16
F32 = jnp.float32
WEST, EAST, SOUTH, NORTH = 0, 1, 2, 3


def kernel(
    lons,
    lats,
    conc_in,
    wind_in,
    kappa_in,
    observed_in,
    conc_to,
    kappa_to,
    grad_conc,
    grad_kappa,
    conc,
    middle,
    lam2,
    lam1,
    own0,
    oth0,
    own1,
    oth1,
    own2,
    oth2,
    wind,
    kappa,
    observed,
    lon_out,
    lon_in,
    lat_out,
    lat_in,
    row_in,
    face_out,
    face_in,
    load_sem,
    lon_send,
    lon_recv,
    lat_send,
    lat_recv,
    early_send,
    early_recv,
    store_sem,
):
    rows, cols, levels = conc_in.shape
    lon, lat = lax.axis_index("lon"), lax.axis_index("lat")
    places = (
        {"lon": lax.rem(lon + lons - 1, lons)},
        {"lon": lax.rem(lon + 1, lons)},
        {"lat": lax.rem(lat + lats - 1, lats)},
        {"lat": lax.rem(lat + 1, lats)},
    )
    loads = [
        pltpu.make_async_copy(
            conc_in, conc.at[pl.ds(1, rows), pl.ds(PAD, cols)], load_sem.at[0]
        ),
        pltpu.make_async_copy(kappa_in, kappa, load_sem.at[1]),
        pltpu.make_async_copy(wind_in, wind, load_sem.at[2]),
        pltpu.make_async_copy(observed_in, observed, load_sem.at[3]),
    ]
    for load in loads:
        load.start()

    barrier = pltpu.get_barrier_semaphore()
    for place in places:
        pl.semaphore_signal(barrier, inc=1, device_id=place, device_id_type=MESH)
    pl.semaphore_wait(barrier, 4)

    def remote(source, target, send, recv, place):
        copy = pltpu.make_async_remote_copy(
            src_ref=source,
            dst_ref=target,
            send_sem=send,
            recv_sem=recv,
            device_id=place,
            device_id_type=MESH,
        )
        copy.start()
        return copy

    started = []
    row_copies = [
        remote(
            wind_in.at[0, rows - 1], row_in.at[0], early_send.at[0], early_recv.at[0], places[EAST]
        ),
        remote(
            kappa_in.at[rows - 1], row_in.at[1], early_send.at[1], early_recv.at[1], places[EAST]
        ),
    ]
    started += row_copies

    half = cols // 2

    def send_lon(state, turn, part):
        inner, there = pl.ds(PAD + part * half, half), pl.ds(part * half, half)
        copies = []
        for way, row in ((EAST, rows), (WEST, 1)):
            lon_out[turn, way, there] = state[row, inner].astype(jnp.bfloat16)
            copies.append(
                remote(
                    lon_out.at[turn, way, there],
                    lon_in.at[turn, way, there],
                    lon_send.at[turn, way, part],
                    lon_recv.at[turn, way, part],
                    places[way],
                )
            )
        started.extend(copies)
        return copies

    def send_lat(state, turn):
        copies = []
        for way, col in ((SOUTH, PAD), (NORTH, PAD + cols - 1)):
            for i in range(rows):
                lat_out[turn, way - 2, i : i + 1] = state[i + 1, col : col + 1]
            copies.append(
                remote(
                    lat_out.at[turn, way - 2],
                    lat_in.at[turn, way - 2],
                    lat_send.at[turn, way - 2],
                    lat_recv.at[turn, way - 2],
                    places[way],
                )
            )
        started.extend(copies)
        return copies

    north_open = (lat < lats - 1).astype(F32)

    def take_lon(state, turn, part, copies):
        for copy in copies:
            copy.wait_recv()
        inner, there = pl.ds(PAD + part * half, half), pl.ds(part * half, half)
        state[rows + 1, inner] = lon_in[turn, WEST, there].astype(F32)
        state[0, inner] = lon_in[turn, EAST, there].astype(F32)

    def take_lat(state, turn, copies):
        for copy in copies:
            copy.wait_recv()
        for i in range(rows):
            edge = state[i + 1, PAD + cols - 1 : PAD + cols]
            ghost = lat_in[turn, 0, i : i + 1]
            state[i + 1, PAD + cols : PAD + cols + 1] = edge + (ghost - edge) * north_open
            state[i + 1, PAD - 1 : PAD] = lat_in[turn, 1, i : i + 1]

    def pair(speed, diffuse):
        return jnp.maximum(speed, 0.0) + diffuse, jnp.minimum(speed, 0.0) - diffuse

    def aligned(start):
        return start if isinstance(start, int) else pl.multiple_of(start, 8)

    def upper(width):
        return (lax.broadcasted_iota(jnp.int32, (width, levels), 1) < levels - 1).astype(F32)

    def chunks(first, last, width, work, most):
        count = (last - first) // width
        group = max(g for g in range(1, most + 1) if count % g == 0)

        def one(t, carry):
            for g in range(group):
                work(pl.multiple_of(first + (t * group + g) * width, width))
            return carry

        if count == group:
            for g in range(group):
                work(first + g * width)
        else:
            lax.fori_loop(0, count // group, one, 0)

    def up(value):
        return pltpu.roll(value, levels - 1, 1)

    def down(value):
        return pltpu.roll(value, 1, 1)

    loads[0].wait()
    lon_copies = [send_lon(conc, 0, part) for part in (0, 1)]
    lat_copies = send_lat(conc, 0)

    loads[1].wait()
    loads[2].wait()

    def coefs_at(j):
        here = pl.ds(j, TILE)
        padded = pl.ds(aligned(j + PAD), TILE)
        shut = upper(TILE)
        for i in range(rows):
            diffuse = kappa[i, here].astype(F32)
            own, oth = pair(wind[0, i, here].astype(F32), diffuse)
            own0[i + 1, here] = own
            oth0[i + 1, here] = oth
            own, oth = pair(wind[1, i, here].astype(F32), diffuse)
            own1[i, padded] = own
            oth1[i, padded] = oth
            own, oth = pair(wind[2, i, here].astype(F32), diffuse)
            own2[i, here] = own * shut
            oth2[i, here] = oth * shut

    chunks(0, cols, TILE, coefs_at, 2)
    last = PAD + cols - 1
    for i in range(rows):
        for place, table in enumerate((own1, oth1)):
            edge = table[i, last : last + 1] * north_open
            table[i, last : last + 1] = edge
            face_out[place, i : i + 1] = edge
    face_copy = remote(face_out, face_in, early_send.at[2], early_recv.at[2], places[NORTH])
    started.append(face_copy)

    def forward(state, target, minus, span, j, width):
        here = pl.ds(j, width)
        mid = aligned(j + PAD)
        at, south, north = pl.ds(mid, width), pl.ds(mid - 1, width), pl.ds(mid + 1, width)
        begin = span[0]
        c = state[begin + 1, at]
        f0_west = own0[begin, here] * state[begin, at] + oth0[begin, here] * c
        for i in span:
            east = state[i + 2, at]
            f0 = own0[i + 1, here] * c + oth0[i + 1, here] * east
            f1 = own1[i, at] * c + oth1[i, at] * state[i + 1, north]
            f1_south = own1[i, south] * state[i + 1, south] + oth1[i, south] * c
            f2 = own2[i, here] * c + oth2[i, here] * up(c)
            new = c - (f0 + f1 + f2) + (f0_west + f1_south + down(f2))
            if minus is not None:
                new = new - minus[i, here].astype(F32)
            target[i + 1, at] = new
            f0_west = f0
            c = east

    def backward(state, c_state, target, lead, add, span, j, width):
        here = pl.ds(j, width)
        mid = aligned(j + PAD)
        at, south, north = pl.ds(mid, width), pl.ds(mid - 1, width), pl.ds(mid + 1, width)
        spot = here if lead == 0 else at
        shut = upper(width)
        begin = span[0]
        lam = state[begin + 1, at]
        c = c_state[begin + 1, at]
        q0_west = oth0[begin, here] * (lam - state[begin, at])
        for i in span:
            lam_east, c_east = state[i + 2, at], c_state[i + 2, at]
            g0 = lam_east - lam
            g1 = state[i + 1, north] - lam
            g2 = up(lam) - lam
            k = g0 * (c - c_east) + g1 * (c - c_state[i + 1, north]) + g2 * (c - up(c)) * shut
            grad_kappa[i, here] = grad_kappa[i, here] + k if add else k
            gained = own0[i + 1, here] * g0 + own1[i, at] * g1 + own2[i, here] * g2
            q1_south = oth1[i, south] * (lam - state[i + 1, south])
            q2 = oth2[i, here] * g2
            target[i + lead, spot] = lam + gained + (q0_west + q1_south + down(q2))
            q0_west = oth0[i + 1, here] * g0
            lam, c = lam_east, c_east

    inside = tuple(range(1, rows - 1))

    def interior(step):
        chunks(TILE, cols - TILE, TILE, lambda j: step(inside, j, TILE), 4)

    def sides(step):
        step(inside, 0, TILE)
        step(inside, cols - TILE, TILE)

    def ends(step, part):
        def both(j):
            step((0,), j, TILE)
            step((rows - 1,), j, TILE)

        chunks(part * half, (part + 1) * half, TILE, both, 7)

    first = functools.partial(forward, conc, middle, None)
    second = functools.partial(forward, middle, lam2, observed)
    third = functools.partial(backward, lam2, middle, lam1, 1, False)
    fourth = functools.partial(backward, lam1, conc, grad_conc, 0, True)

    stores = []

    def store(row, count, col, width, slot):
        where = (pl.ds(row, count), pl.ds(col, width))
        for n, (source, target) in enumerate(((grad_conc, conc_to), (grad_kappa, kappa_to))):
            copy = pltpu.make_async_copy(
                source.at[where], target.at[where], store_sem.at[n, slot]
            )
            copy.start()
            stores.append(copy)

    interior(first)
    face_copy.wait_recv()
    for i in range(rows):
        own1[i, PAD - 1 : PAD] = face_in[0, i : i + 1]
        oth1[i, PAD - 1 : PAD] = face_in[1, i : i + 1]
    take_lat(conc, 0, lat_copies)
    sides(first)
    for copy in row_copies:
        copy.wait_recv()
    own, oth = pair(row_in[0].astype(F32), row_in[1].astype(F32))
    own0[0] = own
    oth0[0] = oth
    for part in (0, 1):
        take_lon(conc, 0, part, lon_copies[part])
        ends(first, part)
        lon_copies[part] = send_lon(middle, 1, part)

    turns = ((middle, second), (lam2, third), (lam1, fourth))
    for turn, (state, step) in enumerate(turns, 1):
        lat_copies = send_lat(state, turn)
        if turn == 1:
            loads[3].wait()
        interior(step)
        take_lat(state, turn, lat_copies)
        sides(step)
        if turn == 3:
            store(1, rows - 2, 0, cols, 0)
        for part in (0, 1):
            take_lon(state, turn, part, lon_copies[part])
            ends(step, part)
            if turn == 3:
                store(0, 1, part * half, half, 1 + part)
                store(rows - 1, 1, part * half, half, 3 + part)
            else:
                lon_copies[part] = send_lon(turns[turn][0], turn + 1, part)

    for copy in stores:
        copy.wait()
    for copy in started:
        copy.wait_send()


def body(lons, lats, concentration, wind, kappa, observed):
    rows, cols, levels = concentration.shape
    state = pltpu.VMEM((rows + 2, cols + 2 * PAD, levels), F32)
    padded = pltpu.VMEM((rows, cols + 2 * PAD, levels), F32)
    wider = pltpu.VMEM((rows + 1, cols, levels), F32)
    plain = pltpu.VMEM((rows, cols, levels), F32)
    out = jax.ShapeDtypeStruct(concentration.shape, F32)
    results = pl.pallas_call(
        functools.partial(kernel, lons, lats),
        out_shape=(out, out),
        in_specs=[pl.BlockSpec(memory_space=pl.ANY)] * 4,
        out_specs=(pl.BlockSpec(memory_space=pl.ANY),) * 2,
        scratch_shapes=[
            plain,
            plain,
            state,
            state,
            state,
            state,
            wider,
            wider,
            padded,
            padded,
            plain,
            plain,
            pltpu.VMEM(wind.shape, wind.dtype),
            pltpu.VMEM(kappa.shape, kappa.dtype),
            pltpu.VMEM(observed.shape, observed.dtype),
            pltpu.VMEM((4, 2, cols, levels), jnp.bfloat16),
            pltpu.VMEM((4, 2, cols, levels), jnp.bfloat16),
            pltpu.VMEM((4, 2, rows, levels), F32),
            pltpu.VMEM((4, 2, rows, levels), F32),
            pltpu.VMEM((2, cols, levels), jnp.bfloat16),
            pltpu.VMEM((2, rows, levels), F32),
            pltpu.VMEM((2, rows, levels), F32),
            pltpu.SemaphoreType.DMA((4,)),
            pltpu.SemaphoreType.DMA((4, 2, 2)),
            pltpu.SemaphoreType.DMA((4, 2, 2)),
            pltpu.SemaphoreType.DMA((4, 2)),
            pltpu.SemaphoreType.DMA((4, 2)),
            pltpu.SemaphoreType.DMA((3,)),
            pltpu.SemaphoreType.DMA((3,)),
            pltpu.SemaphoreType.DMA((2, 5)),
        ],
        compiler_params=pltpu.CompilerParams(
            collective_id=0, has_side_effects=True, vmem_limit_bytes=60 * 1024 * 1024
        ),
    )(concentration, wind, kappa, observed)

    def hand_over(conc_from, kappa_from, conc_to, kappa_to):
        conc_to[...] = conc_from[...]
        kappa_to[...] = kappa_from[...]

    block = pl.BlockSpec((4, cols, levels), lambda i: (i, 0, 0))
    return pl.pallas_call(
        hand_over,
        grid=(rows // 4,),
        out_shape=(out, out),
        in_specs=[block] * 2,
        out_specs=(block,) * 2,
        compiler_params=pltpu.CompilerParams(vmem_limit_bytes=60 * 1024 * 1024),
    )(*results)


def solution(mesh):
    lons, lats = mesh.shape["lon"], mesh.shape["lat"]
    return jax.shard_map(
        functools.partial(body, lons, lats),
        mesh=mesh,
        in_specs=(
            P("lon", "lat", None),
            P(None, "lon", "lat", None),
            P("lon", "lat", None),
            P("lon", "lat", None),
        ),
        out_specs=(P("lon", "lat", None), P("lon", "lat", None)),
        check_vma=False,
    )
```
